512 devices in a mesh: ctx: 64 (over z, y), head: 8 (over x, core).
Axes of the slice: x: 4, y: 4, z: 16, core: 2. Of those that a mesh axis runs over, the one named last changes fastest.
Arguments:
- queries: bfloat16 [4096, 4096], P('ctx', 'head')
- cache_k: bfloat16 [32768, 1024], P('ctx', 'head')
- cache_v: bfloat16 [32768, 1024], P('ctx', 'head'), may hold values from -6 to 6
- new_k: bfloat16 [4096, 1024], P('ctx', 'head'), may hold values from -6 to 6
- new_v: bfloat16 [4096, 1024], P('ctx', 'head'), may hold values from -6 to 6
- counts: int32 [64], P('ctx'), may hold values from 1 to 64, as said below
- positions: int32 [4096], P('ctx'), may hold values from 0 to 4095, as said below
Outputs:
- attended: bfloat16 [4096, 4096], P(('ctx', 'head'))
The draws below stay inside these ranges and needn't reach their ends.
Inputs may be any that keep to these rules, and one draw needn't show every extreme that they name: `counts`: every index of ctx has at least one live slot; some index has exactly 64. Live slots of ctx index c hold consecutive positions starting right after the last live position of index c - 1 (index 0 starts at 0); positions of other slots are arbitrary.
All inputs are finite; a program needn't handle non-finite values.
Results may differ from the reference program's by a relative error of at most 0.0055.
Values may be sent and summed in bfloat16 or wider, within the bound.
A program may use at most 128 MiB of HBM per device.

```python
import math
import jax
import jax.numpy as jnp
from jax import lax

HEADS = 32
KV_HEADS = 8
HD = 128
CACHE_DEV = 512
NEW_CAP = 64
GROUP = 4
CACHE = 32768
NEW_ROWS = 4096
N_CTX = 64


def owned(key):
    first, second = jax.random.split(key)
    amounts = jax.random.randint(first, (N_CTX,), 1, NEW_CAP + 1)
    busiest = jax.random.randint(second, (), 0, N_CTX)
    return amounts.at[busiest].set(NEW_CAP).astype(jnp.int32)


def draw_queries(key, part):
    key = jax.random.fold_in(key, 11)
    values = 3.0 * jax.random.normal(key, (NEW_ROWS, HEADS * HD), jnp.float32)
    return values.astype(jnp.bfloat16)


def draw_cache_k(key, part):
    key = jax.random.fold_in(key, 12)
    values = jax.random.normal(key, (CACHE, KV_HEADS * HD), jnp.float32)
    return values.astype(jnp.bfloat16)


def draw_counts(key, part):
    return owned(key)


def draw_positions(key, part):
    amounts = owned(key)
    key = jax.random.fold_in(key, 21)
    filler = jax.random.randint(key, (N_CTX, NEW_CAP), 0, NEW_ROWS)
    offsets = jnp.cumsum(amounts) - amounts
    slots = jnp.arange(NEW_CAP, dtype=jnp.int32)
    placed = jnp.where(slots[None, :] < amounts[:, None], offsets[:, None] + slots[None, :], filler)
    return placed.reshape(NEW_ROWS).astype(jnp.int32)


def levels(stream_key, extent, cuts, low, largest):
    gain = 1.0
    for position, parts in cuts:
        heights = jax.random.uniform(jax.random.fold_in(jax.random.fold_in(stream_key, 6), position), (parts,), jnp.float32, low / len(cuts), largest / len(cuts))
        gain = gain * jnp.repeat(jnp.exp(heights), extent[position] // parts).reshape((-1,) + (1,) * (len(extent) - 1 - position))
    return gain


def scatter_about(stream_key, shape, scale, most, cuts=(), kind=jnp.bfloat16):
    drawn = jax.random.normal(stream_key, shape, jnp.float32) * scale
    if len(cuts) > 0:
        drawn = levels(stream_key, shape, cuts, -0.22, 0.18) * drawn
    return jnp.clip(drawn, min=-most, max=most).astype(kind)


def setup_inputs(seed: int = 0) -> dict:
    streams_of = jax.random.split(jax.random.key(seed), 8)
    queries = draw_queries(jax.random.fold_in(streams_of[7], 71), 0)
    cache_k = draw_cache_k(jax.random.fold_in(streams_of[7], 71), 0)
    cache_v = scatter_about(streams_of[2], (CACHE, KV_HEADS * HD), 1.0, 6.0, ((0, 64), (1, 8)))
    new_k = scatter_about(streams_of[3], (NEW_ROWS, KV_HEADS * HD), 1.0, 6.0, ((0, 64), (1, 8)))
    new_v = scatter_about(streams_of[4], (NEW_ROWS, KV_HEADS * HD), 1.0, 6.0, ((0, 64), (1, 8)))
    counts = draw_counts(jax.random.fold_in(streams_of[7], 71), 0)
    positions = draw_positions(jax.random.fold_in(streams_of[7], 71), 0)
    return {"queries": queries, "cache_k": cache_k, "cache_v": cache_v, "new_k": new_k, "new_v": new_v, "counts": counts, "positions": positions}


def absorb(best, denom, numer, scores, vals):
    best_new = jnp.maximum(best, lax.optimization_barrier(jnp.max(scores, axis=-1)))
    factor = jnp.exp(best - best_new)
    weights = jnp.exp(scores - best_new[..., None])
    denom = denom * factor + lax.optimization_barrier(jnp.sum(weights, axis=-1))
    rounded = lax.optimization_barrier(weights.astype(jnp.bfloat16))
    contrib = jnp.einsum('rgk,kd->rgd', rounded.astype(jnp.float32), vals.astype(jnp.float32))
    numer = numer * factor[..., None] + contrib
    return (best_new, denom, numer)

def reference(queries, cache_k, cache_v, new_k, new_v, counts, positions):
    scale = 1.0 / math.sqrt(HD)
    rowid = jnp.arange(NEW_ROWS, dtype=jnp.int32)
    live = rowid % NEW_CAP < counts[rowid // NEW_CAP]
    visible = live[None, :] & (positions[None, :] <= positions[:, None])
    qheads = queries.reshape(NEW_ROWS, KV_HEADS, GROUP, HD).transpose(1, 0, 2, 3)
    kcache = cache_k.reshape(N_CTX, CACHE_DEV, KV_HEADS, HD).transpose(2, 0, 1, 3)
    vcache = cache_v.reshape(N_CTX, CACHE_DEV, KV_HEADS, HD).transpose(2, 0, 1, 3)
    knew = new_k.reshape(NEW_ROWS, KV_HEADS, HD).transpose(1, 0, 2)
    vnew = new_v.reshape(NEW_ROWS, KV_HEADS, HD).transpose(1, 0, 2)

    def one_head(items):
        qrows, kblocks, vblocks, kn, vn = items
        qf = qrows.astype(jnp.float32)

        def step(carry, blocks):
            best, denom, numer = carry
            kb, vb = blocks
            scores = jnp.einsum('rgd,kd->rgk', qf, kb.astype(jnp.float32)) * scale
            return (absorb(best, denom, numer, scores, vb), None)
        init = (jnp.full((NEW_ROWS, GROUP), -jnp.inf, jnp.float32), jnp.zeros((NEW_ROWS, GROUP), jnp.float32), jnp.zeros((NEW_ROWS, GROUP, HD), jnp.float32))
        (best, denom, numer), _ = lax.scan(step, init, (kblocks, vblocks))
        scores = jnp.einsum('rgd,kd->rgk', qf, kn.astype(jnp.float32)) * scale
        scores = jnp.where(visible[:, None, :], scores, -jnp.inf)
        best, denom, numer = absorb(best, denom, numer, scores, vn)
        return numer / denom[..., None]
    result = lax.map(one_head, (qheads, kcache, vcache, knew, vnew))
    result = result.transpose(1, 0, 2, 3).reshape(NEW_ROWS, HEADS * HD)
    return jnp.where(live[:, None], result, 0.0).astype(jnp.bfloat16)
```

```python
import functools
import math

import jax
import jax.numpy as jnp
from jax import lax
from jax.experimental import pallas as pl
from jax.experimental.pallas import tpu as pltpu
from jax.sharding import PartitionSpec as P

HD = 128
NY = 4
MESH = pl.DeviceIdType.MESH
F32 = jnp.float32
BF16 = jnp.bfloat16
LOW = -1e30
PIECES = 2


def kernel(
    nz, nh, q_ref, ck_ref, cv_ref, nk_ref, nv_ref, count_ref, pos_ref, out_ref,
    qall, kk, vbuf, nvbuf, vt, bias, scores, probs,
    st_num, st_stat, pin, min_, pout, mout, give, got,
    qsend, qrecv, ysend, yrecv, fsend, frecv, psend, precv, msend, mrecv, asend, arecv,
):
    slots = q_ref.shape[0]
    group = q_ref.shape[1] // HD
    rows = slots * group
    deep = ck_ref.shape[0]
    old = NY * deep
    near = nz // 4
    keys = old + NY * slots
    part = rows // PIECES
    depth = HD // PIECES
    tile = 2 * HD
    ctx = lax.axis_index("ctx")
    head = lax.axis_index("head")
    z = ctx // NY
    y = lax.rem(ctx, NY)

    def wrap(value):
        return lax.rem(value + 2 * nz, nz)

    def at_z(value):
        return (wrap(value) * NY + y, head)

    def at_y(value):
        return (z * NY + lax.rem(value + NY, NY), head)

    def remote(src, dst, send, recv, device):
        return pltpu.make_async_remote_copy(
            src_ref=src, dst_ref=dst, send_sem=send, recv_sem=recv, device_id=device, device_id_type=MESH
        )

    barrier = pltpu.get_barrier_semaphore()
    friends = [at_z(z + 1), at_z(z - 1), at_z(z + near + 1), at_z(z - near - 1), at_y(y + 1), at_y(y - 1)]
    friends += [(ctx, lax.rem(head + k, nh)) for k in range(1, nh)]
    for friend in friends:
        pl.semaphore_signal(barrier, inc=1, device_id=friend, device_id_type=MESH)

    count = count_ref[0]
    own = jnp.concatenate([q_ref[:, g * HD : (g + 1) * HD].astype(F32) for g in range(group)], axis=0)
    qall[z] = own.T.astype(BF16)
    live = lax.broadcasted_iota(jnp.int32, (slots, HD), 0) < count
    newk = nk_ref[...].astype(F32)
    kk[old : old + slots, :] = jnp.where(live, newk, jnp.broadcast_to(newk[0:1, :], newk.shape)).astype(BF16)
    nvbuf[0, :, 0:HD] = jnp.where(live, nv_ref[...].astype(F32), 0.0).astype(BF16)
    nvbuf[0, :, HD:] = jnp.where(live, 1.0, 0.0).astype(BF16)
    pl.semaphore_wait(barrier, len(friends))

    def kv_part(i, k):
        if i == 0:
            return kk.at[k * deep : (k + 1) * deep, :] if k else ck_ref
        if i == 1:
            return kk.at[old + k * slots : old + (k + 1) * slots, :]
        if i == 2:
            return vbuf.at[k] if k else cv_ref
        return nvbuf.at[k]

    def y_copy(way, i):
        device = at_y(y + 1) if way == 0 else at_y(y - 1)
        return remote(kv_part(i, 0), kv_part(i, 1 + way), ysend.at[way, i], yrecv.at[way, i], device)

    def f_copy(i):
        device = at_y(y + 1) if i < 2 else at_y(y - 1)
        return remote(kv_part(i, 1 if i < 2 else 2), kv_part(i, 3), fsend.at[i], frecv.at[i], device)

    def q_copy(way, lane, step, piece, owner, hop=1):
        device = at_z(z + hop) if way == 0 else at_z(z - hop)
        ref = qall.at[owner, pl.ds(piece * depth, depth), :]
        return remote(ref, ref, qsend.at[way, lane, step, piece], qrecv.at[way, lane, step, piece], device)

    for i in range(4):
        for way in (0, 1):
            if i == 0:
                for piece in range(PIECES):
                    q_copy(way, 0, 0, piece, z).start()
                for piece in range(PIECES):
                    q_copy(way, 1, 0, piece, z, near + 1).start()
            y_copy(way, i).start()

    def values_in(k, values_of):
        span = slice(k * deep, (k + 1) * deep)
        vt[0:HD, span] = values_of[...].astype(F32).T.astype(BF16)

    rate = math.log2(math.e) / math.sqrt(HD)

    def attend(one, two, kinds, first, last):
        wide = jnp.concatenate([qall[one], qall[two]], axis=1)
        before = jnp.concatenate([st_stat[one, 0:1, :], st_stat[two, 0:1, :]], axis=1)
        scores[first:last, :] = jnp.dot(kk[first:last, :], wide, preferred_element_type=F32)
        top = jnp.broadcast_to(before, (8, 2 * rows))
        for j in range(first // tile, last // tile):
            here = scores[j * tile : (j + 1) * tile, :]
            if j * tile >= old:
                here = here + jnp.concatenate([bias[kinds[0]], bias[kinds[1]]], axis=1)
                scores[j * tile : (j + 1) * tile, :] = here
            for i in range(0, tile, 8):
                top = jnp.maximum(top, here[i : i + 8])
        top = jnp.max(top, axis=0, keepdims=True)
        for j in range(first // tile, last // tile):
            here = scores[j * tile : (j + 1) * tile, :]
            probs[j * tile : (j + 1) * tile, :] = jnp.exp2((here - top) * rate).astype(BF16)
        both = jnp.dot(vt[:, first:last], probs[first:last, :], preferred_element_type=F32)
        fade = jnp.exp2((before - top) * rate)
        for owner, cols in ((one, slice(0, rows)), (two, slice(rows, 2 * rows))):
            st_num[owner] = st_num[owner] * fade[:, cols] + both[0:HD, cols]
            st_stat[owner, 1:2, :] = st_stat[owner, 1:2, :] * fade[:, cols] + both[HD : HD + 1, cols]
            st_stat[owner, 0:1, :] = top[:, cols]

    def open_blocks(one, two):
        for owner in (one, two):
            st_num[owner] = jnp.zeros((HD, rows), F32)
            st_stat[owner] = jnp.where(lax.broadcasted_iota(jnp.int32, (8, rows), 0) == 0, LOW, 0.0)
        attend(one, two, (0, 0), 0, deep)

    kk[0:deep, :] = ck_ref[...]
    values_in(0, cv_ref)
    vt[HD:, 0:old] = jnp.ones((16, old), BF16)
    line = lax.broadcasted_iota(jnp.int32, (NY * slots, rows), 0)
    which = line // slots
    key_y = y + jnp.where(which == 0, 0, jnp.where(which == 1, NY - 1, which - 1))
    key_y = jnp.where(key_y >= NY, key_y - NY, key_y)
    query_pos = jnp.broadcast_to(jnp.concatenate([pos_ref[...].astype(F32)] * group, axis=1), (rows, rows))
    same = (which == 0) & (line < count) & (query_pos.T <= query_pos)
    bias[0] = jnp.zeros((NY * slots, rows), F32)
    bias[1] = jnp.full((NY * slots, rows), -jnp.inf, F32)
    bias[2] = jnp.where((key_y < y) | same, 0.0, -jnp.inf)
    empty = jnp.where(lax.broadcasted_iota(jnp.int32, (HD + 16, part), 0) == HD, LOW, 0.0).astype(BF16)
    for piece in range(PIECES):
        for lane in (0, 1):
            pin[lane, 0, piece] = empty
            min_[lane, 0, piece] = empty
        min_[1, 1, piece] = empty

    line = lax.broadcasted_iota(jnp.int32, (16, part), 0)

    def state_of(owner, piece):
        here = slice(piece * part, (piece + 1) * part)
        return st_num[owner, :, here], st_stat[owner, 1:2, here], st_stat[owner, 0:1, here]

    def merge(state, message):
        num, den, top = state
        stat = message[HD:].astype(F32)
        top_in = stat[0:1] + stat[1:2] + stat[2:3]
        den_in = stat[3:4] + stat[4:5] + stat[5:6]
        best = jnp.maximum(top, top_in)
        mine = jnp.exp2((top - best) * rate)
        theirs = jnp.exp2((top_in - best) * rate)
        return num * mine + message[0:HD].astype(F32) * theirs, den * mine + den_in * theirs, best

    def three(value):
        one = value.astype(BF16).astype(F32)
        two = (value - one).astype(BF16).astype(F32)
        return one, two, value - one - two

    def message_of(state):
        num, den, top = state
        stat = jnp.zeros((16, part), F32)
        for k, value in enumerate(three(top) + three(den)):
            stat = jnp.where(line == k, value, stat)
        return num.astype(BF16), stat.astype(BF16)

    def hop_of(lane, step):
        return 1 if lane == 0 else jnp.where(step == near - 1, near + 1, 1)

    def p_copy(lane, step, piece):
        return remote(
            pout.at[lane, step, piece], pin.at[lane, step + 1, piece],
            psend.at[lane, step, piece], precv.at[lane, step + 1, piece], at_z(z + hop_of(lane, step)),
        )

    def m_copy(lane, step, piece):
        return remote(
            mout.at[lane, step, piece], min_.at[lane, step + 1, piece],
            msend.at[lane, step, piece], mrecv.at[lane, step + 1, piece], at_z(z - hop_of(lane, step)),
        )

    def turn(step, carry):
        back = step - near

        def kind_of(owner):
            return jnp.where(owner == z, 2, jnp.where(z < owner, 0, 1))

        def p_step(lane, piece):
            owner = wrap(z + near * (lane + 1) - back)
            num, stat = message_of(merge(state_of(owner, piece), pin[lane, back, piece]))
            pout[lane, back, piece, 0:HD, :] = num
            pout[lane, back, piece, HD:, :] = stat
            p_copy(lane, back, piece).start()

        def m_step(lane, piece):
            owner = wrap(z - near * (lane + 1) + back)
            num, stat = message_of(merge(state_of(owner, piece), min_[lane, back, piece]))
            mout[lane, back, piece, 0:HD, :] = num
            mout[lane, back, piece, HD:, :] = stat
            m_copy(lane, back, piece).start()

        @pl.when(step < near)
        def _():
            for lane in (0, 1):
                below_z = wrap(z - step - 1 - lane * near)
                above_z = wrap(z + step + 1 + lane * near)
                for piece in range(PIECES):
                    q_copy(0, lane, step, piece, below_z).wait_recv()

                    @pl.when(step + 1 < near)
                    def _():
                        q_copy(0, lane, step + 1, piece, below_z).start()

                    @pl.when(step + lane < near)
                    def _():
                        q_copy(1, lane, step, piece, above_z).wait_recv()

                    @pl.when(step + 1 + lane < near)
                    def _():
                        q_copy(1, lane, step + 1, piece, above_z).start()

        @pl.when(step >= near)
        def _():
            for lane in (1, 0):
                for piece in range(PIECES):

                    @pl.when(back >= 1)
                    def _():
                        p_copy(lane, back - 1, piece).wait_recv()

                    p_step(lane, piece)

                    @pl.when(back >= 1 + lane)
                    def _():
                        m_copy(lane, back - 1, piece).wait_recv()

                    @pl.when(back >= lane)
                    def _():
                        m_step(lane, piece)

        @pl.when(step == min(1, near - 2))
        def _():
            for i in (0, 1):
                y_copy(0, i).wait_recv()
                f_copy(i).start()

        @pl.when(step == min(2, near - 2))
        def _():
            for i in (2, 3):
                y_copy(1, i).wait_recv()
                f_copy(i).start()
            for i in (2, 3):
                y_copy(0, i).wait_recv()
            values_in(1, vbuf.at[1])
            for i in (0, 1):
                y_copy(1, i).wait_recv()
            values_in(2, vbuf.at[2])

        @pl.when(step == near - 1)
        def _():
            for i in range(4):
                f_copy(i).wait_recv()
            values_in(3, vbuf.at[3])
            turned = jnp.concatenate([nvbuf[k].astype(F32) for k in range(NY)], axis=0).T.astype(BF16)
            vt[:, old:keys] = turned[0 : HD + 16, :]

        @pl.when(step < near)
        def _():
            def open_pair(lane, carry):
                far = step + 1 + lane * near
                open_blocks(wrap(z - far), jnp.where(far == 2 * near, z, wrap(z + far)))
                return carry

            lax.fori_loop(0, 2, open_pair, 0)

        @pl.when((step >= near - 1) & (step < 2 * near - 1))
        def _():
            ahead = step - near + 1

            def rest(which, carry):
                one = jnp.where(ahead == 0, 2 * near, near - ahead)
                two = jnp.where(ahead == 0, near, ahead - near)
                three = jnp.where(ahead == 0, -near, ahead - 2 * near)
                four = jnp.where(ahead == near - 1, 0, 2 * near - 1 - ahead)
                one = wrap(z + jnp.where(which == 0, one, three))
                two = wrap(z + jnp.where(which == 0, two, four))
                attend(one, two, (kind_of(one), kind_of(two)), deep, keys)
                return carry

            lax.fori_loop(0, 2, rest, 0)

        return carry

    lax.fori_loop(0, 2 * near, turn, 0)

    home = []
    for piece in range(PIECES):
        state = state_of(z, piece)
        for lane in (0, 1):
            p_copy(lane, near - 1, piece).wait_recv()
            state = merge(state, pin[lane, near, piece])
            m_copy(lane, near - 1, piece).wait_recv()
            state = merge(state, min_[lane, near, piece])
        num, den, _ = state
        home.append(num / den)
    place = lax.broadcasted_iota(jnp.int32, (rows, HD), 0) % slots
    result = jnp.where(place < count, jnp.concatenate(home, axis=1).T, 0.0)

    take = slots // nh
    for j in range(nh):
        block = [result[g * slots + j * take : g * slots + (j + 1) * take] for g in range(group)]
        if take < 16:
            wide = [jnp.concatenate(block[: group // 2], axis=1), jnp.concatenate(block[group // 2 :], axis=1)]
            give[j] = jnp.concatenate(wide, axis=0).astype(BF16)
        else:
            give[j] = jnp.concatenate(block, axis=1).astype(BF16)

    def a_copy(k, to, slot_there):
        return remote(give.at[to], got.at[slot_there], asend.at[k], arecv.at[k], (ctx, to))

    for k in range(1, nh):
        a_copy(k, lax.rem(head + k, nh), head).start()
    got[head] = give[head]
    for k in range(1, nh):
        a_copy(k, lax.rem(head + k, nh), lax.rem(head + nh - k, nh)).wait_recv()
    out = []
    for j in range(nh):
        block = got[j].astype(F32)
        out += [block[0:take], block[take:]] if take < 16 else [block]
    out_ref[...] = jnp.concatenate(out, axis=1).astype(BF16)

    for k in range(1, nh):
        a_copy(k, lax.rem(head + k, nh), head).wait_send()
    for way in (0, 1):
        for i in range(4):
            y_copy(way, i).wait_send()
        for lane in (0, 1):
            for step in range(near - way * lane):
                for piece in range(PIECES):
                    q_copy(way, lane, step, piece, z).wait_send()
    for i in range(4):
        f_copy(i).wait_send()

    for lane in (0, 1):
        for step in range(near):
            for piece in range(PIECES):
                p_copy(lane, step, piece).wait_send()
                if step >= lane:
                    m_copy(lane, step, piece).wait_send()


def solution(mesh):
    n_ctx, nh = mesh.shape["ctx"], mesh.shape["head"]
    nz = n_ctx // NY
    near = nz // 4

    def local(queries, cache_k, cache_v, new_k, new_v, counts, positions):
        slots = queries.shape[0]
        group = queries.shape[1] // HD
        rows = slots * group
        deep = cache_k.shape[0]
        keys = NY * (deep + slots)
        take = slots // nh
        block = (2 * take, group * HD // 2) if take < 16 else (take, group * HD)
        message = (PIECES, HD + 16, rows // PIECES)
        vmem = pl.BlockSpec(memory_space=pltpu.VMEM)
        dma = pltpu.SemaphoreType.DMA
        return pl.pallas_call(
            functools.partial(kernel, nz, nh),
            out_shape=jax.ShapeDtypeStruct((take, nh * group * HD), BF16),
            in_specs=[vmem] * 5 + [pl.BlockSpec(memory_space=pltpu.SMEM), vmem],
            out_specs=vmem,
            scratch_shapes=[
                pltpu.VMEM((nz, HD, rows), BF16),
                pltpu.VMEM((keys, HD), BF16),
                pltpu.VMEM((NY, deep, HD), BF16),
                pltpu.VMEM((NY, slots, 2 * HD), BF16),
                pltpu.VMEM((HD + 16, keys), BF16),
                pltpu.VMEM((3, NY * slots, rows), F32),
                pltpu.VMEM((keys, 2 * rows), F32),
                pltpu.VMEM((keys, 2 * rows), BF16),
                pltpu.VMEM((nz, HD, rows), F32),
                pltpu.VMEM((nz, 8, rows), F32),
                pltpu.VMEM((2, near + 1) + message, BF16),
                pltpu.VMEM((2, near + 1) + message, BF16),
                pltpu.VMEM((2, near) + message, BF16),
                pltpu.VMEM((2, near) + message, BF16),
                pltpu.VMEM((nh,) + block, BF16),
                pltpu.VMEM((nh,) + block, BF16),
                dma((2, 2, near, PIECES)),
                dma((2, 2, near, PIECES)),
                dma((2, 4)),
                dma((2, 4)),
                dma((4,)),
                dma((4,)),
                dma((2, near, PIECES)),
                dma((2, near + 1, PIECES)),
                dma((2, near, PIECES)),
                dma((2, near + 1, PIECES)),
                dma((nh,)),
                dma((nh,)),
            ],
            compiler_params=pltpu.CompilerParams(
                collective_id=0, has_side_effects=True, vmem_limit_bytes=56 * 1024 * 1024
            ),
        )(
            queries, cache_k, cache_v, new_k, new_v, counts,
            positions.reshape(1, slots),
        )

    spec = P("ctx", "head")
    return jax.shard_map(
        local,
        mesh=mesh,
        in_specs=(spec, spec, spec, spec, spec, P("ctx"), P("ctx")),
        out_specs=P(("ctx", "head"), None),
        check_vma=False,
    )
```

```python
import functools
import math

import jax
import jax.numpy as jnp
from jax import lax
from jax.experimental import pallas as pl
from jax.experimental.pallas import tpu as pltpu
from jax.sharding import PartitionSpec as P

HD = 128
NY = 4
MESH = pl.DeviceIdType.MESH
F32 = jnp.float32
BF16 = jnp.bfloat16
LOW = -1e30
PIECES = 2
CHUNK = 64


def kernel(
    nz, nh, q_ref, ck_ref, cv_ref, nk_ref, nv_ref, count_ref, pos_ref, out_ref,
    qall, kk, vbuf, nvbuf, vt, bias, scores, probs,
    st_num, st_stat, pin, min_, pout, mout, give, got,
    qsend, qrecv, ysend, yrecv, fsend, frecv, psend, precv, msend, mrecv, asend, arecv,
):
    slots = q_ref.shape[0]
    group = q_ref.shape[1] // HD
    rows = slots * group
    deep = ck_ref.shape[0]
    old = NY * deep
    near = nz // 4
    keys = old + NY * slots
    part = rows // PIECES
    depth = HD // PIECES
    ctx = lax.axis_index("ctx")
    head = lax.axis_index("head")
    z = ctx // NY
    y = lax.rem(ctx, NY)

    def wrap(value):
        return lax.rem(value + 2 * nz, nz)

    def at_z(value):
        return (wrap(value) * NY + y, head)

    def at_y(value):
        return (z * NY + lax.rem(value + NY, NY), head)

    def remote(src, dst, send, recv, device):
        return pltpu.make_async_remote_copy(
            src_ref=src, dst_ref=dst, send_sem=send, recv_sem=recv, device_id=device, device_id_type=MESH
        )

    barrier = pltpu.get_barrier_semaphore()
    friends = [at_z(z + 1), at_z(z - 1), at_z(z + near + 1), at_z(z - near - 1), at_y(y + 1), at_y(y - 1)]
    friends += [(ctx, lax.rem(head + k, nh)) for k in range(1, nh)]
    for friend in friends:
        pl.semaphore_signal(barrier, inc=1, device_id=friend, device_id_type=MESH)

    count = count_ref[0]
    own = jnp.concatenate([q_ref[:, g * HD : (g + 1) * HD].astype(F32) for g in range(group)], axis=0)
    qall[z] = own.T.astype(BF16)
    live = lax.broadcasted_iota(jnp.int32, (slots, HD), 0) < count
    newk = nk_ref[...].astype(F32)
    kk[old : old + slots, :] = jnp.where(live, newk, jnp.broadcast_to(newk[0:1, :], newk.shape)).astype(BF16)
    nvbuf[0, :, 0:HD] = jnp.where(live, nv_ref[...].astype(F32), 0.0).astype(BF16)
    nvbuf[0, :, HD:] = jnp.where(live, 1.0, 0.0).astype(BF16)
    pl.semaphore_wait(barrier, len(friends))

    def kv_part(i, k):
        if i == 0:
            return kk.at[k * deep : (k + 1) * deep, :] if k else ck_ref
        if i == 1:
            return kk.at[old + k * slots : old + (k + 1) * slots, :]
        if i == 2:
            return vbuf.at[k] if k else cv_ref
        return nvbuf.at[k]

    def y_copy(way, i):
        device = at_y(y + 1) if way == 0 else at_y(y - 1)
        return remote(kv_part(i, 0), kv_part(i, 1 + way), ysend.at[way, i], yrecv.at[way, i], device)

    def f_copy(i):
        device = at_y(y + 1) if i < 2 else at_y(y - 1)
        return remote(kv_part(i, 1 if i < 2 else 2), kv_part(i, 3), fsend.at[i], frecv.at[i], device)

    def q_copy(way, lane, step, piece, owner, hop=1):
        device = at_z(z + hop) if way == 0 else at_z(z - hop)
        ref = qall.at[owner, pl.ds(piece * depth, depth), :]
        return remote(ref, ref, qsend.at[way, lane, step, piece], qrecv.at[way, lane, step, piece], device)

    for i in range(4):
        for way in (0, 1):
            if i == 0:
                for piece in range(PIECES):
                    q_copy(way, 0, 0, piece, z).start()
                for piece in range(PIECES):
                    q_copy(way, 1, 0, piece, z, near + 1).start()
            y_copy(way, i).start()

    def values_in(k, values_of):
        span = slice(k * deep, (k + 1) * deep)
        vt[0:HD, span] = values_of[...].astype(F32).T.astype(BF16)

    rate = math.log2(math.e) / math.sqrt(HD)

    def attend(one, two, kinds, first, last):
        wide = jnp.concatenate([qall[one], qall[two]], axis=1)
        before = jnp.concatenate([st_stat[one, 0:1, :], st_stat[two, 0:1, :]], axis=1)
        scores[first:last, :] = jnp.dot(kk[first:last, :], wide, preferred_element_type=F32)
        top = jnp.broadcast_to(before, (8, 2 * rows))
        for j in range(first, last, CHUNK):
            here = scores[j : j + CHUNK, :]
            if j >= old:
                hidden = [bias[kind, j - old : j - old + CHUNK, :] for kind in kinds]
                here = here + jnp.concatenate(hidden, axis=1)
                scores[j : j + CHUNK, :] = here
            for i in range(0, CHUNK, 8):
                top = jnp.maximum(top, here[i : i + 8])
        top = jnp.max(top, axis=0, keepdims=True)
        for j in range(first, last, CHUNK):
            probs[j : j + CHUNK, :] = jnp.exp2((scores[j : j + CHUNK, :] - top) * rate).astype(BF16)
        both = jnp.dot(vt[:, first:last], probs[first:last, :], preferred_element_type=F32)
        fade = jnp.exp2((before - top) * rate)
        for owner, cols in ((one, slice(0, rows)), (two, slice(rows, 2 * rows))):
            st_num[owner] = st_num[owner] * fade[:, cols] + both[0:HD, cols]
            st_stat[owner, 1:2, :] = st_stat[owner, 1:2, :] * fade[:, cols] + both[HD : HD + 1, cols]
            st_stat[owner, 0:1, :] = top[:, cols]

    def open_blocks(one, two):
        for owner in (one, two):
            st_num[owner] = jnp.zeros((HD, rows), F32)
            st_stat[owner] = jnp.where(lax.broadcasted_iota(jnp.int32, (8, rows), 0) == 0, LOW, 0.0)
        attend(one, two, (0, 0), 0, deep)

    kk[0:deep, :] = ck_ref[...]
    values_in(0, cv_ref)
    vt[HD:, 0:old] = jnp.ones((16, old), BF16)
    line = lax.broadcasted_iota(jnp.int32, (NY * slots, rows), 0)
    which = line // slots
    key_y = y + jnp.where(which == 0, 0, jnp.where(which == 1, NY - 1, which - 1))
    key_y = jnp.where(key_y >= NY, key_y - NY, key_y)
    query_pos = jnp.broadcast_to(jnp.concatenate([pos_ref[...].astype(F32)] * group, axis=1), (rows, rows))
    same = (which == 0) & (line < count) & (query_pos.T <= query_pos)
    bias[0] = jnp.zeros((NY * slots, rows), F32)
    bias[1] = jnp.full((NY * slots, rows), -jnp.inf, F32)
    bias[2] = jnp.where((key_y < y) | same, 0.0, -jnp.inf)
    empty = jnp.where(lax.broadcasted_iota(jnp.int32, (HD + 16, part), 0) == HD, LOW, 0.0).astype(BF16)
    for piece in range(PIECES):
        for lane in (0, 1):
            pin[lane, 0, piece] = empty
            min_[lane, 0, piece] = empty
        min_[1, 1, piece] = empty

    line = lax.broadcasted_iota(jnp.int32, (16, part), 0)

    def state_of(owner, piece):
        here = slice(piece * part, (piece + 1) * part)
        return st_num[owner, :, here], st_stat[owner, 1:2, here], st_stat[owner, 0:1, here]

    def merge(state, message):
        num, den, top = state
        stat = message[HD:].astype(F32)
        top_in = stat[0:1] + stat[1:2] + stat[2:3]
        den_in = stat[3:4] + stat[4:5] + stat[5:6]
        best = jnp.maximum(top, top_in)
        mine = jnp.exp2((top - best) * rate)
        theirs = jnp.exp2((top_in - best) * rate)
        return num * mine + message[0:HD].astype(F32) * theirs, den * mine + den_in * theirs, best

    def three(value):
        one = value.astype(BF16).astype(F32)
        two = (value - one).astype(BF16).astype(F32)
        return one, two, value - one - two

    def message_of(state):
        num, den, top = state
        stat = jnp.zeros((16, part), F32)
        for k, value in enumerate(three(top) + three(den)):
            stat = jnp.where(line == k, value, stat)
        return num.astype(BF16), stat.astype(BF16)

    def hop_of(lane, step):
        return 1 if lane == 0 else jnp.where(step == near - 1, near + 1, 1)

    def p_copy(lane, step, piece):
        return remote(
            pout.at[lane, step, piece], pin.at[lane, step + 1, piece],
            psend.at[lane, step, piece], precv.at[lane, step + 1, piece], at_z(z + hop_of(lane, step)),
        )

    def m_copy(lane, step, piece):
        return remote(
            mout.at[lane, step, piece], min_.at[lane, step + 1, piece],
            msend.at[lane, step, piece], mrecv.at[lane, step + 1, piece], at_z(z - hop_of(lane, step)),
        )

    def turn(step, carry):
        back = step - near

        def kind_of(owner):
            return jnp.where(owner == z, 2, jnp.where(z < owner, 0, 1))

        def p_step(lane, piece):
            owner = wrap(z + near * (lane + 1) - back)
            num, stat = message_of(merge(state_of(owner, piece), pin[lane, back, piece]))
            pout[lane, back, piece, 0:HD, :] = num
            pout[lane, back, piece, HD:, :] = stat
            p_copy(lane, back, piece).start()

        def m_step(lane, piece):
            owner = wrap(z - near * (lane + 1) + back)
            num, stat = message_of(merge(state_of(owner, piece), min_[lane, back, piece]))
            mout[lane, back, piece, 0:HD, :] = num
            mout[lane, back, piece, HD:, :] = stat
            m_copy(lane, back, piece).start()

        @pl.when(step < near)
        def _():
            for lane in (0, 1):
                below_z = wrap(z - step - 1 - lane * near)
                above_z = wrap(z + step + 1 + lane * near)
                for piece in range(PIECES):
                    q_copy(0, lane, step, piece, below_z).wait_recv()

                    @pl.when(step + 1 < near)
                    def _():
                        q_copy(0, lane, step + 1, piece, below_z).start()

                    @pl.when(step + lane < near)
                    def _():
                        q_copy(1, lane, step, piece, above_z).wait_recv()

                    @pl.when(step + 1 + lane < near)
                    def _():
                        q_copy(1, lane, step + 1, piece, above_z).start()

        @pl.when(step >= near)
        def _():
            for lane in (1, 0):
                for piece in range(PIECES):

                    @pl.when(back >= 1)
                    def _():
                        p_copy(lane, back - 1, piece).wait_recv()

                    p_step(lane, piece)

                    @pl.when(back >= 1 + lane)
                    def _():
                        m_copy(lane, back - 1, piece).wait_recv()

                    @pl.when(back >= lane)
                    def _():
                        m_step(lane, piece)

        @pl.when(step == min(1, near - 2))
        def _():
            for i in (0, 1):
                y_copy(0, i).wait_recv()
                f_copy(i).start()

        @pl.when(step == min(2, near - 2))
        def _():
            for i in (2, 3):
                y_copy(1, i).wait_recv()
                f_copy(i).start()
            for i in (2, 3):
                y_copy(0, i).wait_recv()
            values_in(1, vbuf.at[1])
            for i in (0, 1):
                y_copy(1, i).wait_recv()
            values_in(2, vbuf.at[2])

        @pl.when(step == near - 1)
        def _():
            for i in range(4):
                f_copy(i).wait_recv()
            values_in(3, vbuf.at[3])
            turned = jnp.concatenate([nvbuf[k].astype(F32) for k in range(NY)], axis=0).T.astype(BF16)
            vt[:, old:keys] = turned[0 : HD + 16, :]

        @pl.when(step < near)
        def _():
            def open_pair(lane, carry):
                far = step + 1 + lane * near
                open_blocks(wrap(z - far), jnp.where(far == 2 * near, z, wrap(z + far)))
                return carry

            lax.fori_loop(0, 2, open_pair, 0)

        @pl.when((step >= near - 1) & (step < 2 * near - 1))
        def _():
            ahead = step - near + 1

            def rest(which, carry):
                one = jnp.where(ahead == 0, 2 * near, near - ahead)
                two = jnp.where(ahead == 0, near, ahead - near)
                three = jnp.where(ahead == 0, -near, ahead - 2 * near)
                four = jnp.where(ahead == near - 1, 0, 2 * near - 1 - ahead)
                one = wrap(z + jnp.where(which == 0, one, three))
                two = wrap(z + jnp.where(which == 0, two, four))
                attend(one, two, (kind_of(one), kind_of(two)), deep, keys)
                return carry

            lax.fori_loop(0, 2, rest, 0)

        return carry

    lax.fori_loop(0, 2 * near, turn, 0)

    home = []
    for piece in range(PIECES):
        state = state_of(z, piece)
        for lane in (0, 1):
            p_copy(lane, near - 1, piece).wait_recv()
            state = merge(state, pin[lane, near, piece])
            m_copy(lane, near - 1, piece).wait_recv()
            state = merge(state, min_[lane, near, piece])
        num, den, _ = state
        home.append(num / den)
    place = lax.broadcasted_iota(jnp.int32, (rows, HD), 0) % slots
    result = jnp.where(place < count, jnp.concatenate(home, axis=1).T, 0.0)

    take = slots // nh
    for j in range(nh):
        block = [result[g * slots + j * take : g * slots + (j + 1) * take] for g in range(group)]
        if take < 16:
            wide = [jnp.concatenate(block[: group // 2], axis=1), jnp.concatenate(block[group // 2 :], axis=1)]
            give[j] = jnp.concatenate(wide, axis=0).astype(BF16)
        else:
            give[j] = jnp.concatenate(block, axis=1).astype(BF16)

    def a_copy(k, to, slot_there):
        return remote(give.at[to], got.at[slot_there], asend.at[k], arecv.at[k], (ctx, to))

    for k in range(1, nh):
        a_copy(k, lax.rem(head + k, nh), head).start()
    got[head] = give[head]
    for k in range(1, nh):
        a_copy(k, lax.rem(head + k, nh), lax.rem(head + nh - k, nh)).wait_recv()
    out = []
    for j in range(nh):
        block = got[j].astype(F32)
        out += [block[0:take], block[take:]] if take < 16 else [block]
    out_ref[...] = jnp.concatenate(out, axis=1).astype(BF16)

    for k in range(1, nh):
        a_copy(k, lax.rem(head + k, nh), head).wait_send()
    for way in (0, 1):
        for i in range(4):
            y_copy(way, i).wait_send()
        for lane in (0, 1):
            for step in range(near - way * lane):
                for piece in range(PIECES):
                    q_copy(way, lane, step, piece, z).wait_send()
    for i in range(4):
        f_copy(i).wait_send()

    for lane in (0, 1):
        for step in range(near):
            for piece in range(PIECES):
                p_copy(lane, step, piece).wait_send()
                if step >= lane:
                    m_copy(lane, step, piece).wait_send()


def solution(mesh):
    n_ctx, nh = mesh.shape["ctx"], mesh.shape["head"]
    nz = n_ctx // NY
    near = nz // 4

    def local(queries, cache_k, cache_v, new_k, new_v, counts, positions):
        slots = queries.shape[0]
        group = queries.shape[1] // HD
        rows = slots * group
        deep = cache_k.shape[0]
        keys = NY * (deep + slots)
        take = slots // nh
        block = (2 * take, group * HD // 2) if take < 16 else (take, group * HD)
        message = (PIECES, HD + 16, rows // PIECES)
        vmem = pl.BlockSpec(memory_space=pltpu.VMEM)
        dma = pltpu.SemaphoreType.DMA
        return pl.pallas_call(
            functools.partial(kernel, nz, nh),
            out_shape=jax.ShapeDtypeStruct((take, nh * group * HD), BF16),
            in_specs=[vmem] * 5 + [pl.BlockSpec(memory_space=pltpu.SMEM), vmem],
            out_specs=vmem,
            scratch_shapes=[
                pltpu.VMEM((nz, HD, rows), BF16),
                pltpu.VMEM((keys, HD), BF16),
                pltpu.VMEM((NY, deep, HD), BF16),
                pltpu.VMEM((NY, slots, 2 * HD), BF16),
                pltpu.VMEM((HD + 16, keys), BF16),
                pltpu.VMEM((3, NY * slots, rows), F32),
                pltpu.VMEM((keys, 2 * rows), F32),
                pltpu.VMEM((keys, 2 * rows), BF16),
                pltpu.VMEM((nz, HD, rows), F32),
                pltpu.VMEM((nz, 8, rows), F32),
                pltpu.VMEM((2, near + 1) + message, BF16),
                pltpu.VMEM((2, near + 1) + message, BF16),
                pltpu.VMEM((2, near) + message, BF16),
                pltpu.VMEM((2, near) + message, BF16),
                pltpu.VMEM((nh,) + block, BF16),
                pltpu.VMEM((nh,) + block, BF16),
                dma((2, 2, near, PIECES)),
                dma((2, 2, near, PIECES)),
                dma((2, 4)),
                dma((2, 4)),
                dma((4,)),
                dma((4,)),
                dma((2, near, PIECES)),
                dma((2, near + 1, PIECES)),
                dma((2, near, PIECES)),
                dma((2, near + 1, PIECES)),
                dma((nh,)),
                dma((nh,)),
            ],
            compiler_params=pltpu.CompilerParams(
                collective_id=0, has_side_effects=True, vmem_limit_bytes=56 * 1024 * 1024
            ),
        )(
            queries, cache_k, cache_v, new_k, new_v, counts,
            positions.reshape(1, slots),
        )

    spec = P("ctx", "head")
    return jax.shard_map(
        local,
        mesh=mesh,
        in_specs=(spec, spec, spec, spec, spec, P("ctx"), P("ctx")),
        out_specs=P(("ctx", "head"), None),
        check_vma=False,
    )
```
